256 devices in a mesh: dp: 32 (over z, x), mp: 8 (over y, core).
Axes of the slice: x: 4, y: 4, z: 8, core: 2. Of those that a mesh axis runs over, the one named last changes fastest.
Arguments:
- activations: bfloat16 [32, 1024, 3072], P('dp', 'mp'), may hold values from -6 to 6
- cotangent: bfloat16 [32, 1024, 3072], P('dp', None, 'mp'), may hold values from -0.19921875 to 0.19921875
- weight: bfloat16 [3072, 3072], P(None, 'mp'), may hold values from -3 to 3
- feedback: bfloat16 [32, 3072, 3072], P('dp', None, 'mp'), may hold values from -3 to 3
- q_previous: float32 [3072, 64], P('mp'), may hold values from -6 to 6
Outputs:
- input_grad: bfloat16 [32, 1024, 3072], P('dp', 'mp')
- p_basis: float32 [3072, 64], replicated
- q_factor: float32 [3072, 64], P('mp')
- feedback_new: bfloat16 [32, 3072, 3072], P('dp', None, 'mp')
The draws below stay inside these ranges and needn't reach their ends.
All inputs are finite; a program needn't handle non-finite values.
Results may differ from the reference program's by a relative error of at most 0.02.
Values may be sent and summed in bfloat16 or wider, within the bound.
No kernel may reach another device: no remote copies, remote signals or barrier semaphores. Data moves between devices by JAX's collectives and lax.ppermute only.
A program may use at most 128 MiB of HBM per device.

```python
import jax
import jax.numpy as jnp
from jax import lax

D = 3072
OUT = 3072
RANK = 64
TOKENS = 1024
REPLICAS = 32
N_DP = 32


def block_levels(rng, dims, shards, low, high):
    factor_of, own = 1.0, jax.random.fold_in(rng, 6)
    for axis_at, parts in shards:
        heights = jnp.exp(jax.random.uniform(jax.random.fold_in(own, axis_at), (parts,), jnp.float32, low / len(shards), high / len(shards)))
        factor_of = factor_of * jnp.repeat(heights, dims[axis_at] // parts).reshape([-1 if axis == axis_at else 1 for axis in range(len(dims))])
    return factor_of


def normal_values(rng, dims, scale, limit, cuts=(), dtype=jnp.bfloat16):
    values = scale * jax.random.normal(rng, dims, jnp.float32)
    if cuts:
        values = values * block_levels(rng, dims, cuts, -0.22, 0.18)
    return jnp.clip(values, -limit, limit).astype(dtype)


def setup_inputs(seed: int = 0) -> dict:
    key_list = jax.random.split(jax.random.key(seed), 6)
    return {
        "activations": normal_values(key_list[0], (REPLICAS, TOKENS, D), 1.0, 6.0, ((0, 32), (1, 8))),
        "cotangent": normal_values(key_list[1], (REPLICAS, TOKENS, OUT), 0.03125, 0.19921875, ((0, 32), (2, 8))),
        "weight": normal_values(key_list[2], (D, OUT), 4 ** -0.5, 3.0, ((1, 8),)),
        "feedback": normal_values(key_list[3], (REPLICAS, D, OUT), 0.5, 3.0, ((0, 32), (2, 8))),
        "q_previous": normal_values(key_list[4], (OUT, RANK), 1.0, 6.0, ((0, 8),), jnp.float32),
    }


def reference(activations, cotangent, weight, feedback, q_previous):
    q_low = q_previous.astype(jnp.bfloat16)

    def merge_one(triple):
        act_rows, cot_rows, old_feedback = triple
        gradient = jnp.dot(act_rows.T.astype(jnp.float32), cot_rows.astype(jnp.float32), preferred_element_type=jnp.float32)
        merged = (gradient + old_feedback.astype(jnp.float32)).astype(jnp.bfloat16)
        return (merged, jnp.dot(merged.astype(jnp.float32), q_low.astype(jnp.float32), preferred_element_type=jnp.float32))
    merged_all, p_terms = lax.map(merge_one, (activations, cotangent, feedback))
    p_summed = jnp.sum(p_terms, axis=0)
    gram_matrix = jnp.dot(p_summed.T.astype(jnp.float32), p_summed.astype(jnp.float32), precision=lax.Precision.HIGHEST, preferred_element_type=jnp.float32)
    lower_factor = jnp.linalg.cholesky(gram_matrix)
    p_basis = lax.linalg.triangular_solve(lower_factor, p_summed, left_side=False, lower=True, transpose_a=True)
    basis_low = p_basis.astype(jnp.bfloat16)
    q_terms = lax.map(lambda merged: jnp.dot(merged.T.astype(jnp.float32), basis_low.astype(jnp.float32), preferred_element_type=jnp.float32), merged_all)
    q_factor = jnp.sum(q_terms, axis=0) / N_DP
    approx = jnp.dot(p_basis.astype(jnp.float32), q_factor.T.astype(jnp.float32), precision=lax.Precision.HIGHEST, preferred_element_type=jnp.float32)
    feedback_new = lax.map(lambda merged: (merged.astype(jnp.float32) - approx).astype(jnp.bfloat16), merged_all)
    input_grad = lax.map(lambda cot_rows: jnp.dot(cot_rows.astype(jnp.float32), weight.T.astype(jnp.float32), preferred_element_type=jnp.float32).astype(jnp.bfloat16), cotangent)
    return (input_grad, p_basis, q_factor, feedback_new)
```

```python
import functools

import jax
import jax.numpy as jnp
from jax import lax
from jax.experimental import pallas as pl
from jax.experimental.pallas import tpu as pltpu
from jax.sharding import Mesh, PartitionSpec as P

F32 = jnp.float32
BF16 = jnp.bfloat16
NX, NY, NZ, NC = 4, 4, 8, 2
MP = ("y", "c")
XYC = ("x", "y", "c")


def ring(value, axis, size, shift):
    return lax.ppermute(value, axis, [(i, (i + shift) % size) for i in range(size)])


def exchange(value, axes):
    return lax.all_to_all(value, axes, 0, 0, tiled=True)


def spread(value, axes, count):
    return exchange(jnp.broadcast_to(value[None], (count,) + value.shape), axes)


def split(value):
    high = lax.reduce_precision(value, 8, 7)
    return high.astype(BF16), (value - high).astype(BF16)


def merge_kernel(*refs):
    acts, cot_ref, old_ref, out_ref = refs[:8], refs[8], refs[9], refs[10]
    rows = jnp.concatenate([ref[...] for ref in acts], axis=0)
    gradient = lax.dot_general(
        rows, cot_ref[...], (((0,), (0,)), ((), ())), preferred_element_type=F32
    )
    out_ref[...] = (gradient + old_ref[...].astype(F32)).astype(BF16)


def merge(acts, cot_rel, old_feedback):
    d, cols = old_feedback.shape
    rows = acts[0].shape[0]
    tile = 512
    return pl.pallas_call(
        merge_kernel,
        grid=(d // tile,),
        in_specs=[pl.BlockSpec((rows, tile), lambda i: (0, i))] * 8
        + [
            pl.BlockSpec(cot_rel.shape, lambda i: (0, 0)),
            pl.BlockSpec((tile, cols), lambda i: (i, 0)),
        ],
        out_specs=pl.BlockSpec((tile, cols), lambda i: (i, 0)),
        out_shape=jax.ShapeDtypeStruct((d, cols), BF16),
        compiler_params=pltpu.CompilerParams(vmem_limit_bytes=32 * 2**20),
        cost_estimate=pl.CostEstimate(
            flops=2 * d * cols * rows * 8, bytes_accessed=12 * 2**20, transcendentals=0
        ),
    )(*acts, cot_rel, old_feedback)


def local(activations, cotangent, weight, feedback, q_previous):
    act, cot, old = activations[0], cotangent[0], feedback[0]
    y, c = lax.axis_index("y"), lax.axis_index("c")
    cot_blocks = cot.reshape(NY, NC, 128, 384)

    same = [act] + [ring(act, "y", NY, k) for k in (1, 3, 2)]
    other = [ring(value, "c", NC, 1) for value in same]
    acts = [value for pair in zip(same, other) for value in pair]
    from_y = [(y - k) % NY for k in (0, 1, 3, 2)]
    cot_rel = jnp.concatenate(
        [cot_blocks[yy, cc] for yy in from_y for cc in (c, 1 - c)], axis=0
    )

    q_low = q_previous.astype(BF16)
    t_part = jnp.dot(cot, q_low, preferred_element_type=F32)
    t_send = t_part.reshape(8, 2, 64, 64).transpose(0, 2, 1, 3).reshape(8, 64, 128)
    t_sum = exchange(t_send, MP).sum(0)
    t_rows = jnp.concatenate([t_sum[:, :64], t_sum[:, 64:]], axis=0)
    t_high, t_low = split(t_rows)
    contract = (((0,), (0,)), ((), ()))
    p_part = (
        lax.dot_general(act, t_high, contract, preferred_element_type=F32)
        + lax.dot_general(act, t_low, contract, preferred_element_type=F32)
        + jnp.dot(old, q_low, preferred_element_type=F32)
    )
    p_send = jnp.concatenate([p_part[:1536], p_part[1536:]], axis=1).reshape(32, 48, 128)
    p_chunk = exchange(p_send, XYC).sum(0)
    p_chunk = exchange(jnp.broadcast_to(p_chunk[None], (NZ, 48, 128)), "z").sum(0)
    p_all = spread(p_chunk, XYC, 32).reshape(1536, 128)
    p_summed = jnp.concatenate([p_all[:, :64], p_all[:, 64:]], axis=0)

    merged = merge(acts, cot_rel, old)

    p_high, p_low = split(p_summed)
    s_part = lax.dot_general(p_high, merged, contract, preferred_element_type=F32)
    s_part += lax.dot_general(p_low, merged, contract, preferred_element_type=F32)
    s_send = s_part.reshape(64, 3, 128).transpose(1, 0, 2).reshape(NX, 48, 128)
    s_chunk = exchange(s_send, "x").sum(0)
    s_chunk = spread(s_chunk, "z", NZ).sum(0)
    s_all = spread(s_chunk, "x", NX).reshape(3, 64, 128).transpose(1, 0, 2).reshape(64, 384)

    gram_matrix = jnp.dot(
        p_summed.T, p_summed, precision=lax.Precision.HIGHEST, preferred_element_type=F32
    )
    lower_factor = jnp.linalg.cholesky(gram_matrix)
    p_basis = lax.linalg.triangular_solve(
        lower_factor, p_summed, left_side=False, lower=True, transpose_a=True
    )
    q_t = lax.linalg.triangular_solve(lower_factor, s_all, left_side=True, lower=True) / 32
    approx = jnp.dot(p_basis, q_t, precision=lax.Precision.HIGHEST, preferred_element_type=F32)
    feedback_new = (merged.astype(F32) - approx).astype(BF16)

    to_t = (((1,), (1,)), ((), ()))
    for_other = lax.dot_general(
        cot_blocks[:, 1 - c].reshape(512, 384), weight, to_t, preferred_element_type=F32
    ).astype(BF16)
    got = ring(for_other, "c", NC, 1)
    mine = lax.dot_general(
        cot_blocks[:, c].reshape(512, 384), weight, to_t, preferred_element_type=F32
    )
    chip = (mine + got.astype(F32)).astype(BF16).reshape(NY, 128, 3072)
    chip, *_ = lax.optimization_barrier((chip, *same))
    total = chip[y].astype(F32)
    for k in (1, 3, 2):
        total += ring(chip[(y + k) % NY], "y", NY, k).astype(F32)
    input_grad = total.astype(BF16)
    return input_grad[None], p_basis, q_t.T, feedback_new[None]


def solution(mesh):
    fine = Mesh(mesh.devices.reshape(NZ, NX, NY, NC), ("z", "x", "y", "c"))
    dp = ("z", "x")
    placed = (P(dp, MP, None), P(dp, None, MP), P(None, MP), P(dp, None, MP), P(MP, None))
    return jax.shard_map(
        local,
        mesh=fine,
        in_specs=placed,
        out_specs=(P(dp, MP, None), P(), P(MP, None), P(dp, None, MP)),
        check_vma=False,
    )
```

```python
import functools

import jax
import jax.numpy as jnp
from jax import lax
from jax.experimental import pallas as pl
from jax.experimental.pallas import tpu as pltpu
from jax.sharding import Mesh, PartitionSpec as P

F32 = jnp.float32
BF16 = jnp.bfloat16
NX, NY, NZ, NC = 4, 4, 8, 2
DP, MP = ("z", "x"), ("y", "c")
N_DP = NZ * NX
HALF, COLS, RANK, BLOCK, D = 1536, 384, 64, 128, 3072
TILE = 512
STEPS = HALF // TILE
HIGHEST = lax.Precision.HIGHEST


def ring(value, axis, size, shift):
    return lax.ppermute(value, axis, [(i, (i + shift) % size) for i in range(size)])


def exchange(value, axes):
    return lax.all_to_all(value, axes, 0, 0, tiled=True)


def call(kernel, outs, flops, grid=None, **kwargs):
    return pl.pallas_call(
        kernel,
        out_shape=outs,
        compiler_params=pltpu.CompilerParams(vmem_limit_bytes=40 * 2**20),
        cost_estimate=pl.CostEstimate(
            flops=int(flops), bytes_accessed=4 * 2**20, transcendentals=0
        ),
        **({} if grid is None else {"grid": grid}),
        **kwargs,
    )


def out(shape, dtype=F32):
    return jax.ShapeDtypeStruct(shape, dtype)


def dot(a, b, dims=((1,), (0,)), precision=None):
    return lax.dot_general(a, b, (dims, ((), ())), precision=precision, preferred_element_type=F32)


def two(value):
    high = value.astype(BF16)
    return high, (value - high.astype(F32)).astype(BF16)


def lanes(shape):
    return lax.broadcasted_iota(jnp.int32, shape, 1)


def sides(q):
    zero = jnp.zeros_like(q)
    return jnp.concatenate([q, zero], axis=1), jnp.concatenate([zero, q], axis=1)


def t_kernel(cot_ref, q_ref, out_ref):
    left, right = sides(q_ref[...].astype(BF16))
    cot = cot_ref[...].reshape(8, 2, 64, COLS)
    first, second = cot[:, 0].reshape(512, COLS), cot[:, 1].reshape(512, COLS)
    out_ref[...] = (dot(first, left) + dot(second, right)).reshape(8, 64, 128)


def t_rows(cot, q):
    return call(t_kernel, out((8, 64, 128)), 2e8)(cot, q)


def f_kernel(old_ref, q_ref, first_ref, second_ref, fq_ref, act_ref):
    left, right = sides(q_ref[...].astype(BF16))
    fq_ref[...] = dot(old_ref[0], left) + dot(old_ref[1], right)
    act_ref[0] = first_ref[...].T
    act_ref[1] = second_ref[...].T


def f_rows(old, q, act):
    return call(
        f_kernel,
        [out((HALF, 128)), out((2, HALF, BLOCK), BF16)],
        3e8,
        grid=(STEPS,),
        in_specs=[
            pl.BlockSpec((2, TILE, COLS), lambda i: (0, i, 0)),
            pl.BlockSpec((COLS, RANK), lambda i: (0, 0)),
            pl.BlockSpec((BLOCK, TILE), lambda i: (0, i)),
            pl.BlockSpec((BLOCK, TILE), lambda i: (0, i + STEPS)),
        ],
        out_specs=[
            pl.BlockSpec((TILE, 128), lambda i: (i, 0)),
            pl.BlockSpec((2, TILE, BLOCK), lambda i: (0, i, 0)),
        ],
    )(old, q, act, act)


def p_kernel(t_ref, act_ref, fq_ref, out_ref):
    t = jnp.sum(t_ref[...], axis=0)
    low_lane = lanes(t.shape) < 64
    turned = pltpu.roll(t, 64, 1)
    rhs = jnp.concatenate(
        [
            jnp.where(low_lane, t, 0.0),
            jnp.where(low_lane, turned, 0.0),
            jnp.where(low_lane, 0.0, turned),
            jnp.where(low_lane, 0.0, t),
        ],
        axis=0,
    )
    lhs = jnp.concatenate([act_ref[0], act_ref[1]], axis=1)
    both = dot(lhs, jnp.concatenate(two(rhs), axis=1))
    out_ref[...] = both[:, :128] + both[:, 128:] + fq_ref[...]


def p_rows(t, act, fq):
    return call(p_kernel, out((HALF, 128)), 2e8)(t, act, fq)


def sum_kernel(in_ref, out_ref):
    out_ref[...] = jnp.broadcast_to(jnp.sum(in_ref[...], axis=0)[None], out_ref.shape)


def sum_spread(value, count):
    return call(sum_kernel, out((count,) + value.shape[1:]), 1e6)(value)


def merge_kernel(place_ref, cot_ref, old_ref, *refs):
    acts, (out_ref, cot_rel) = refs[:-2], refs[-2:]
    y, c = place_ref[0], place_ref[1]

    @pl.when(pl.program_id(0) == 0)
    def _():
        for n, k in enumerate((0, 3, 1, 2)):
            for m in range(2):
                block = lax.rem(y + k, NY) * 2 + (c if m == 0 else 1 - c)
                cot_rel[pl.ds((2 * n + m) * BLOCK, BLOCK), :] = cot_ref[
                    pl.ds(pl.multiple_of(block * BLOCK, BLOCK), BLOCK), :
                ]

    for h in range(2):
        near = [ref[h] for ref in acts[:6]]
        far = [ref[...] for ref in acts[6 + 2 * h : 8 + 2 * h]]
        gradient = dot(jnp.concatenate(near + far, axis=1), cot_rel[...])
        out_ref[h] = (gradient + old_ref[h].astype(F32)).astype(BF16)


def merge(place, cot, old, near, far):
    return call(
        merge_kernel,
        out((2, HALF, COLS), BF16),
        2.4e9,
        grid=(STEPS,),
        in_specs=[
            pl.BlockSpec(memory_space=pltpu.SMEM),
            pl.BlockSpec(cot.shape, lambda i: (0, 0)),
            pl.BlockSpec((2, TILE, COLS), lambda i: (0, i, 0)),
        ]
        + [pl.BlockSpec((2, TILE, BLOCK), lambda i: (0, i, 0))] * 6
        + [pl.BlockSpec((TILE, BLOCK), lambda i: (i, 0))] * 4,
        out_specs=pl.BlockSpec((2, TILE, COLS), lambda i: (0, i, 0)),
        scratch_shapes=[pltpu.VMEM((8 * BLOCK, COLS), BF16)],
    )(place, cot, old, *near, *far)


def s_kernel(p_ref, merged_ref, out_ref):
    p = jnp.concatenate(two(p_ref[...]), axis=1)
    first = dot(p, merged_ref[0], ((0,), (0,)))
    second = dot(p, merged_ref[1], ((0,), (0,)))
    s = first[:64] + first[128:192] + second[64:128] + second[192:]
    for n in range(3):
        out_ref[pl.ds(64 * n, 64), :] = s[:, 128 * n : 128 * n + 128]
    out_ref[pl.ds(192, 64), :] = jnp.zeros((64, 128), F32)


def s_rows(p, merged):
    return call(s_kernel, out((256, 128)), 1.2e9)(p, merged)


def basis_kernel(p_ref, basis_ref, packed_ref, inverse_ref):
    p = p_ref[...]
    pair = dot(p, p, ((0,), (0,)), HIGHEST)
    gram = pair[:64, :64] + pair[64:, 64:]
    row = lax.broadcasted_iota(jnp.int32, (64, 64), 0)
    unit = jnp.where(row == lanes((64, 64)), 1.0, 0.0)
    table = jnp.concatenate([gram, unit], axis=1)
    tiles = [table[8 * i : 8 * i + 8] for i in range(8)]
    sub = lax.broadcasted_iota(jnp.int32, (8, 128), 0)
    for j in range(64):
        at, inner = j // 8, j % 8
        pivot = tiles[at][inner : inner + 1]
        scaled = pivot * (1.0 / pivot[:, j : j + 1])
        for i in range(at, 8):
            factor = jnp.broadcast_to(tiles[i][:, j : j + 1], (8, 128))
            if i == at:
                factor = jnp.where(sub > inner, factor, 0.0)
            tiles[i] = tiles[i] - factor * scaled
    table = jnp.concatenate(tiles, axis=0)
    lane = lanes((64, 128))
    here = lax.broadcasted_iota(jnp.int32, (64, 128), 0) == lane
    diagonal = jnp.sum(jnp.where(here, table, 0.0), axis=1, keepdims=True)
    right = jnp.where(lane >= 64, table, 0.0) / jnp.sqrt(diagonal)
    inverse = jnp.concatenate([pltpu.roll(right, 64, 1), right], axis=0)
    basis = dot(p, inverse, ((1,), (1,)), HIGHEST)
    inverse_ref[...] = inverse
    packed_ref[...] = basis
    basis_ref[0] = basis[:, :64]
    basis_ref[1] = basis[:, 64:]


def basis_rows(p):
    return call(
        basis_kernel, [out((2, HALF, 64)), out((HALF, 128)), out((128, 128))], 5e9
    )(p)


def last_kernel(s_ref, inverse_ref, packed_ref, merged_ref, q_ref, new_ref, rhs):
    @pl.when(pl.program_id(0) == 0)
    def _():
        s = jnp.concatenate([s_ref[pl.ds(64 * n, 64), :] for n in range(3)], axis=1)
        q = dot(inverse_ref[0:64, 0:64], s, precision=HIGHEST) * (1.0 / N_DP)
        q_ref[...] = q.T
        high, low = two(q)
        zero = jnp.zeros_like(high)
        for h in range(2):
            pair = lambda v: [zero, v] if h else [v, zero]
            rhs[h] = jnp.concatenate(pair(high) + pair(high) + pair(low), axis=0)

    high, low = two(packed_ref[...])
    lhs = jnp.concatenate([high, low, high], axis=1)
    for h in range(2):
        new_ref[h] = (merged_ref[h].astype(F32) - dot(lhs, rhs[h])).astype(BF16)


def last(s, inverse, packed, merged):
    return call(
        last_kernel,
        [out((COLS, RANK)), out((2, HALF, COLS), BF16)],
        1e9,
        grid=(STEPS,),
        in_specs=[
            pl.BlockSpec((256, 128), lambda i: (0, 0)),
            pl.BlockSpec((128, 128), lambda i: (0, 0)),
            pl.BlockSpec((TILE, 128), lambda i: (i, 0)),
            pl.BlockSpec((2, TILE, COLS), lambda i: (0, i, 0)),
        ],
        out_specs=[
            pl.BlockSpec((COLS, RANK), lambda i: (0, 0)),
            pl.BlockSpec((2, TILE, COLS), lambda i: (0, i, 0)),
        ],
        scratch_shapes=[pltpu.VMEM((2, 384, COLS), BF16)],
    )(s, inverse, packed, merged)


def pick(place_ref, cot_ref, own):
    y, c = place_ref[0], place_ref[1]
    core = c if own else 1 - c
    rows = [
        cot_ref[
            pl.ds(pl.multiple_of((lax.rem(y + k, NY) * 2 + core) * BLOCK, BLOCK), BLOCK), :
        ]
        for k in range(NY)
    ]
    return jnp.concatenate(rows, axis=0)


def other_kernel(place_ref, cot_ref, weight_ref, out_ref):
    part = dot(pick(place_ref, cot_ref, False), weight_ref[...], ((1,), (1,)))
    out_ref[...] = part.astype(BF16)


def own_kernel(place_ref, cot_ref, weight_ref, got_ref, *out_refs):
    part = dot(pick(place_ref, cot_ref, True), weight_ref[...], ((1,), (1,)))
    part = (part + got_ref[...].astype(F32)).astype(BF16)
    for k, ref in enumerate(out_refs):
        ref[...] = part[k * BLOCK : (k + 1) * BLOCK]


def grad_specs(cot):
    return [
        pl.BlockSpec(memory_space=pltpu.SMEM),
        pl.BlockSpec(cot.shape, lambda i: (0, 0)),
        pl.BlockSpec((TILE, COLS), lambda i: (i, 0)),
    ]


def grad_other(place, cot, weight):
    return call(
        other_kernel,
        out((NY * BLOCK, D), BF16),
        1.2e9,
        grid=(D // TILE,),
        in_specs=grad_specs(cot),
        out_specs=pl.BlockSpec((NY * BLOCK, TILE), lambda i: (0, i)),
    )(place, cot, weight)


def grad_own(place, cot, weight, got):
    return call(
        own_kernel,
        [out((BLOCK, D), BF16)] * NY,
        1.2e9,
        grid=(D // TILE,),
        in_specs=grad_specs(cot) + [pl.BlockSpec((NY * BLOCK, TILE), lambda i: (0, i))],
        out_specs=[pl.BlockSpec((BLOCK, TILE), lambda i: (0, i))] * NY,
    )(place, cot, weight, got)


def add_kernel(a_ref, b_ref, c_ref, d_ref, out_ref):
    total = a_ref[...].astype(F32) + b_ref[...].astype(F32)
    out_ref[...] = (total + c_ref[...].astype(F32) + d_ref[...].astype(F32)).astype(BF16)


def add_four(parts):
    return call(add_kernel, out((BLOCK, D), BF16), 2e6)(*parts)


def after(values, *earlier):
    held = lax.optimization_barrier((tuple(values), earlier))
    return list(held[0])


def local(activations, cotangent, weight, feedback, q_previous):
    act, cot = activations[0], cotangent[0]
    old = feedback[0].reshape(2, HALF, COLS)
    place = jnp.stack([lax.axis_index("y"), lax.axis_index("c")]).astype(jnp.int32)

    t = exchange(t_rows(cot, q_previous), MP)
    fq, act_t = f_rows(old, q_previous, act)
    p_send = p_rows(t, act_t, fq).reshape(N_DP, 48, 128)

    (near,) = after([act_t], t)
    low, high = ring(near, "y", NY, 1), ring(near, "y", NY, 3)

    p_mp = exchange(sum_spread(exchange(p_send, DP), 8), MP)
    from_low, from_high = after([low[1], high[0]], p_mp)
    far_second, far_first = ring(from_low, "y", NY, 1), ring(from_high, "y", NY, 3)
    p = exchange(sum_spread(p_mp, N_DP), DP).reshape(HALF, 128)

    side = lambda value: ring(value, "c", NC, 1)
    near_all = [near, side(near), low, side(low), high, side(high)]
    far_all = [far_first, side(far_first), far_second, side(far_second)]
    merged = merge(place, cot, old, near_all, far_all)

    got = side(grad_other(place, cot, weight))
    mine, *rest = grad_own(place, cot, weight, got)
    rest = after(rest, far_first, far_second)
    parts = [ring(value, "y", NY, k) for k, value in zip((1, 2, 3), rest)]
    input_grad = add_four([mine] + parts)

    s = exchange(s_rows(p, merged).reshape(N_DP, 8, 128), DP)
    basis, packed, inverse = basis_rows(p)
    s = exchange(sum_spread(s, N_DP), DP).reshape(256, 128)
    q_factor, feedback_new = last(s, inverse, packed, merged)
    return (
        input_grad[None],
        basis.reshape(D, RANK),
        q_factor,
        feedback_new.reshape(1, D, COLS),
    )


def solution(mesh):
    fine = Mesh(mesh.devices.reshape(NZ, NX, NY, NC), ("z", "x", "y", "c"))
    placed = (P(DP, MP, None), P(DP, None, MP), P(None, MP), P(DP, None, MP), P(MP, None))
    return jax.shard_map(
        local,
        mesh=fine,
        in_specs=placed,
        out_specs=(P(DP, MP, None), P(), P(MP, None), P(DP, None, MP)),
        check_vma=False,
    )
```

```python
import functools

import jax
import jax.numpy as jnp
from jax import lax
from jax.experimental import pallas as pl
from jax.experimental.pallas import tpu as pltpu
from jax.sharding import Mesh, PartitionSpec as P

F32 = jnp.float32
BF16 = jnp.bfloat16
NX, NY, NZ, NC = 4, 4, 8, 2
DP, MP, PLANE = ("z", "x"), ("y", "c"), ("x", "y")
N_DP = NZ * NX
HALF, COLS, RANK, BLOCK, D = 1536, 384, 64, 128, 3072
PART = HALF // 2
TILE = 512
STEPS = HALF // TILE
HIGHEST = lax.Precision.HIGHEST


def ring(value, axis, size, shift):
    return lax.ppermute(value, axis, [(i, (i + shift) % size) for i in range(size)])


def exchange(value, axes):
    return lax.all_to_all(value, axes, 0, 0, tiled=True)


def call(kernel, outs, flops, grid=None, pins=(), near=(), prefetch=False, **kwargs):
    if prefetch:
        names = ("in_specs", "out_specs", "scratch_shapes")
        spec = {name: kwargs.pop(name) for name in names if name in kwargs}
        kwargs["grid_spec"] = pltpu.PrefetchScalarGridSpec(
            num_scalar_prefetch=1, grid=grid, **spec
        )
        grid = None
    made = pl.pallas_call(
        kernel,
        out_shape=outs,
        compiler_params=pltpu.CompilerParams(vmem_limit_bytes=16 * 2**20),
        cost_estimate=pl.CostEstimate(
            flops=int(flops), bytes_accessed=1000, transcendentals=0
        ),
        **({} if grid is None else {"grid": grid}),
        **kwargs,
    )
    held = pltpu.with_memory_space_constraint
    where = {n: pltpu.HBM for n in pins} | {n: pltpu.VMEM for n in near}
    return lambda *args: made(
        *(held(v, where[n]) if n in where else v for n, v in enumerate(args))
    )


def out(shape, dtype=F32):
    return jax.ShapeDtypeStruct(shape, dtype)


def far_out(shape, dtype=F32):
    return pltpu.HBM(shape, dtype)


def dot(a, b, dims=((1,), (0,)), precision=None):
    return lax.dot_general(a, b, (dims, ((), ())), precision=precision, preferred_element_type=F32)


def two(value):
    high = value.astype(BF16)
    return high, (value - high.astype(F32)).astype(BF16)


def lanes(shape):
    return lax.broadcasted_iota(jnp.int32, shape, 1)


def sides(q):
    zero = jnp.zeros_like(q)
    return jnp.concatenate([q, zero], axis=0), jnp.concatenate([zero, q], axis=0)


ROWS = ((1,), (1,))


def t_kernel(cot_ref, q_ref, out_ref):
    left, right = sides(q_ref[...].astype(BF16))
    cot = cot_ref[...].reshape(4, 2, 64, COLS)
    first, second = cot[:, 0].reshape(256, COLS), cot[:, 1].reshape(256, COLS)
    both = dot(first, left, ROWS) + dot(second, right, ROWS)
    out_ref[...] = both.reshape(4, 64, 128)


def t_rows(cot, q):
    return call(
        t_kernel,
        out((8, 64, 128)),
        1e3,
        grid=(2,),
        pins=(0, 1),
        in_specs=[
            pl.BlockSpec((512, COLS), lambda i: (i, 0)),
            pl.BlockSpec((RANK, COLS), lambda i: (0, 0)),
        ],
        out_specs=pl.BlockSpec((4, 64, 128), lambda i: (i, 0, 0)),
    )(cot, q)


def f_kernel(old_ref, q_ref, first_ref, second_ref, fq_ref, act0_ref, act1_ref):
    left, right = sides(q_ref[...].astype(BF16))
    fq_ref[...] = dot(old_ref[0], left, ROWS) + dot(old_ref[1], right, ROWS)
    act0_ref[...] = first_ref[...].T
    act1_ref[...] = second_ref[...].T


def f_rows(old, q, act):
    return call(
        f_kernel,
        [far_out((HALF, 128))] + [out((HALF, BLOCK), BF16)] * 2,
        1e3,
        grid=(STEPS,),
        pins=(0, 1, 2, 3),
        in_specs=[
            pl.BlockSpec((2, TILE, COLS), lambda i: (0, i, 0)),
            pl.BlockSpec((RANK, COLS), lambda i: (0, 0)),
            pl.BlockSpec((BLOCK, TILE), lambda i: (0, i)),
            pl.BlockSpec((BLOCK, TILE), lambda i: (0, i + STEPS)),
        ],
        out_specs=[
            pl.BlockSpec((TILE, 128), lambda i: (i, 0)),
            pl.BlockSpec((TILE, BLOCK), lambda i: (i, 0)),
            pl.BlockSpec((TILE, BLOCK), lambda i: (i, 0)),
        ],
    )(old, q, act, act)


def p_kernel(place_ref, t_ref, act0_ref, act1_ref, fq_ref, keep_ref, send_ref):
    t = jnp.sum(t_ref[...], axis=0)
    low_lane = lanes(t.shape) < 64
    turned = pltpu.roll(t, 64, 1)
    rhs = jnp.concatenate(
        [
            jnp.where(low_lane, t, 0.0),
            jnp.where(low_lane, turned, 0.0),
            jnp.where(low_lane, 0.0, turned),
            jnp.where(low_lane, 0.0, t),
        ],
        axis=0,
    )
    lhs = jnp.concatenate([act0_ref[...], act1_ref[...]], axis=1)
    both = dot(lhs, jnp.concatenate(two(rhs), axis=1))
    total = both[:, :128] + both[:, 128:] + fq_ref[...]
    for n, ref in enumerate((keep_ref, send_ref)):

        @pl.when(pl.program_id(0) == n)
        def _():
            ref[...] = total


def half_of(i, place):
    return lax.rem(place[1] + i, 2)


def p_rows(place, t, act0, act1, fq):
    return call(
        p_kernel,
        [out((PART, 128))] * 2,
        1e3,
        grid=(2,),
        pins=(4,),
        prefetch=True,
        in_specs=[
            pl.BlockSpec((8, 64, 128), lambda i, place: (0, 0, 0)),
            pl.BlockSpec((PART, BLOCK), lambda i, place: (half_of(i, place), 0)),
            pl.BlockSpec((PART, BLOCK), lambda i, place: (half_of(i, place), 0)),
            pl.BlockSpec((PART, 128), lambda i, place: (half_of(i, place), 0)),
        ],
        out_specs=[pl.BlockSpec((PART, 128), lambda i, place: (0, 0))] * 2,
    )(place, t, act0, act1, fq)


def pair_kernel(a_ref, b_ref, out_ref):
    out_ref[...] = a_ref[...] + b_ref[...]


def pair_sum(a, b):
    return call(pair_kernel, far_out(a.shape), 1e3)(a, b)


def sum_kernel(in_ref, out_ref):
    total = jnp.sum(in_ref[...].astype(F32), axis=0)
    out_ref[...] = jnp.broadcast_to(total[None], out_ref.shape)


def sum_spread(value, count):
    return call(sum_kernel, out((count,) + value.shape[1:]), 1e3)(value)


def merge_kernel(place_ref, cot_ref, old_ref, *refs):
    acts, (out_ref, cot_rel) = refs[:-2], refs[-2:]
    y, c = place_ref[0], place_ref[1]

    @pl.when(pl.program_id(0) == 0)
    def _():
        for n, k in enumerate((0, 3, 1, 2)):
            for m in range(2):
                block = lax.rem(y + k, NY) * 2 + (c if m == 0 else 1 - c)
                cot_rel[pl.ds((2 * n + m) * BLOCK, BLOCK), :] = cot_ref[
                    pl.ds(pl.multiple_of(block * BLOCK, BLOCK), BLOCK), :
                ]

    for h in range(2):
        rows = jnp.concatenate([ref[...] for ref in acts[8 * h : 8 * h + 8]], axis=1)
        gradient = dot(rows, cot_rel[...])
        out_ref[h] = (gradient + old_ref[h].astype(F32)).astype(BF16)


def merge(place, cot, old, acts):
    return call(
        merge_kernel,
        pltpu.VMEM((2, HALF, COLS), BF16),
        1.5e10,
        grid=(STEPS,),
        pins=tuple(range(1, 19)),
        in_specs=[
            pl.BlockSpec(memory_space=pltpu.SMEM),
            pl.BlockSpec(cot.shape, lambda i: (0, 0)),
            pl.BlockSpec((2, TILE, COLS), lambda i: (0, i, 0)),
        ]
        + [pl.BlockSpec((TILE, BLOCK), lambda i: (i, 0))] * 16,
        out_specs=pl.BlockSpec((2, TILE, COLS), lambda i: (0, i, 0)),
        scratch_shapes=[pltpu.VMEM((8 * BLOCK, COLS), BF16)],
    )(place, cot, old, *acts)


def s_kernel(place_ref, p_ref, merged_ref, before_ref, out_ref):
    p = jnp.concatenate(two(p_ref[...]), axis=1)
    first = dot(p, merged_ref[0], ((0,), (0,)))
    second = dot(p, merged_ref[1], ((0,), (0,)))
    s = first[:64] + first[128:192] + second[64:128] + second[192:]
    for n in range(3):
        at = pl.ds(64 * n, 64)
        out_ref[at, :] = before_ref[at, :] + s[:, 128 * n : 128 * n + 128]
    out_ref[pl.ds(192, 64), :] = before_ref[pl.ds(192, 64), :]


def s_rows(place, p, merged, before, flip):
    return call(
        s_kernel,
        out((256, 128)),
        1e3,
        grid=(1,),
        near=(2,),
        prefetch=True,
        in_specs=[
            pl.BlockSpec((PART, 128), lambda i, place: (0, 0)),
            pl.BlockSpec((2, PART, COLS), lambda i, place: (0, half_of(flip, place), 0)),
            pl.BlockSpec((256, 128), lambda i, place: (0, 0)),
        ],
        out_specs=pl.BlockSpec((256, 128), lambda i, place: (0, 0)),
    )(place, p, merged, before)


def gram_half(p):
    high, rest = p.astype(BF16), p - p.astype(BF16).astype(F32)
    split = jnp.concatenate([high, *two(rest)], axis=1)
    blocks = dot(split, split, ((0,), (0,)))
    part = lambda a, b: blocks[128 * a : 128 * a + 128, 128 * b : 128 * b + 128]
    small = part(0, 2) + part(2, 0) + part(1, 1)
    return part(0, 0) + (part(0, 1) + part(1, 0) + small)


def inverse_kernel(own_ref, other_ref, inverse_ref):
    pair = gram_half(own_ref[...]) + gram_half(other_ref[...])
    gram = pair[:64, :64] + pair[64:, 64:]
    row = lax.broadcasted_iota(jnp.int32, (64, 64), 0)
    unit = jnp.where(row == lanes((64, 64)), 1.0, 0.0)
    table = jnp.concatenate([gram, unit], axis=1)
    tiles = [table[8 * i : 8 * i + 8] for i in range(8)]
    sub = lax.broadcasted_iota(jnp.int32, (8, 128), 0)
    for j in range(0, 64, 4):
        at, inner = j // 8, j % 8
        columns = [
            {i: jnp.broadcast_to(tiles[i][:, j + k : j + k + 1], (8, 128)) for i in range(at, 8)}
            for k in range(4)
        ]
        for k in range(4):
            n = inner + k
            scale = 1.0 / columns[k][at][n : n + 1]
            heads = [columns[m][at][n : n + 1] for m in range(k + 1, 4)]
            pivot = tiles[at][n : n + 1]
            for i in range(at, 8):
                factor = columns[k][i] * scale
                if i == at:
                    factor = jnp.where(sub > n, factor, 0.0)
                for m, head in zip(range(k + 1, 4), heads):
                    columns[m][i] = columns[m][i] - factor * head
                tiles[i] = tiles[i] - factor * pivot
    table = jnp.concatenate(tiles, axis=0)
    lane = lanes((64, 128))
    here = lax.broadcasted_iota(jnp.int32, (64, 128), 0) == lane
    diagonal = jnp.sum(jnp.where(here, table, 0.0), axis=1, keepdims=True)
    right = jnp.where(lane >= 64, table, 0.0) / jnp.sqrt(diagonal)
    inverse_ref[...] = jnp.concatenate([pltpu.roll(right, 64, 1), right], axis=0)


def basis_kernel(place_ref, own_ref, other_ref, inverse_ref, basis_ref, packed_ref):
    inverse = inverse_ref[...]
    for n, ref in enumerate((own_ref, other_ref)):
        half = lax.rem(place_ref[1] + n, 2)
        start = pl.multiple_of(half * PART, PART)
        p = ref[...]
        packed_ref[pl.ds(start, PART), :] = dot(p, inverse, ROWS, HIGHEST)
        turned = dot(inverse, p, ROWS, HIGHEST)
        for h in range(2):
            at = pl.ds(pl.multiple_of(start + h * HALF, PART), PART)
            basis_ref[:, at] = turned[64 * h : 64 * h + 64]


def inverse_rows(own, other):
    return call(inverse_kernel, out((128, 128)), 1e3)(own, other)


def basis_rows(place, own, other, inverse):
    return call(
        basis_kernel,
        [out((RANK, D)), out((HALF, 128))],
        1e3,
        in_specs=[pl.BlockSpec(memory_space=pltpu.SMEM)] + [pl.BlockSpec()] * 3,
    )(place, own, other, inverse)


def last_kernel(s_ref, inverse_ref, packed_ref, merged_ref, q_ref, new_ref, rhs):
    @pl.when(pl.program_id(0) == 0)
    def _():
        s = jnp.concatenate([s_ref[pl.ds(64 * n, 64), :] for n in range(3)], axis=1)
        q = dot(inverse_ref[0:64, 0:64], s, precision=HIGHEST) * (1.0 / N_DP)
        q_ref[...] = q
        high, low = two(q)
        zero = jnp.zeros_like(high)
        for h in range(2):
            pair = lambda v: [zero, v] if h else [v, zero]
            rhs[h] = jnp.concatenate(pair(high) + pair(high) + pair(low), axis=0)

    high, low = two(packed_ref[...])
    lhs = jnp.concatenate([high, low, high], axis=1)
    for h in range(2):
        new_ref[h] = (merged_ref[h].astype(F32) - dot(lhs, rhs[h])).astype(BF16)


def last(s, inverse, packed, merged):
    return call(
        last_kernel,
        [far_out((RANK, COLS)), far_out((2, HALF, COLS), BF16)],
        1e3,
        grid=(STEPS,),
        near=(3,),
        in_specs=[
            pl.BlockSpec((256, 128), lambda i: (0, 0)),
            pl.BlockSpec((128, 128), lambda i: (0, 0)),
            pl.BlockSpec((TILE, 128), lambda i: (i, 0)),
            pl.BlockSpec((2, TILE, COLS), lambda i: (0, i, 0)),
        ],
        out_specs=[
            pl.BlockSpec((RANK, COLS), lambda i: (0, 0)),
            pl.BlockSpec((2, TILE, COLS), lambda i: (0, i, 0)),
        ],
        scratch_shapes=[pltpu.VMEM((2, 384, COLS), BF16)],
    )(s, inverse, packed, merged)


def grad_kernel(place_ref, cot_ref, weight_ref, cot_side_ref, weight_side_ref, *refs):
    out_refs, rows = refs[:-1], refs[-1]

    @pl.when(pl.program_id(0) == 0)
    def _():
        for k in range(NY):
            block = lax.rem(place_ref[0] + k, NY) * 2 + place_ref[1]
            start = pl.multiple_of(block * BLOCK, BLOCK)
            for n, ref in enumerate((cot_ref, cot_side_ref)):
                rows[n * COLS : (n + 1) * COLS, k * BLOCK : (k + 1) * BLOCK] = ref[
                    pl.ds(start, BLOCK), :
                ].T

    weight = jnp.concatenate([weight_ref[...], weight_side_ref[...]], axis=1)
    part = dot(weight, rows[...]).astype(BF16)
    for k, ref in enumerate(out_refs):
        ref[...] = part[:, k * BLOCK : (k + 1) * BLOCK]


def grad_parts(place, cot, cot_side, weight, weight_side):
    whole = pl.BlockSpec(cot.shape, lambda i: (0, 0))
    tile = pl.BlockSpec((TILE, COLS), lambda i: (i, 0))
    return call(
        grad_kernel,
        [far_out((D, BLOCK), BF16)] * NY,
        1e3,
        grid=(D // TILE,),
        pins=(1, 3),
        in_specs=[pl.BlockSpec(memory_space=pltpu.SMEM), whole, tile, whole, tile],
        out_specs=[pl.BlockSpec((TILE, BLOCK), lambda i: (i, 0))] * NY,
        scratch_shapes=[pltpu.VMEM((2 * COLS, NY * BLOCK), BF16)],
    )(place, cot, weight, cot_side, weight_side)


def add_kernel(*refs):
    total = refs[0][...].astype(F32)
    for ref in refs[1:NY]:
        total += ref[...].astype(F32)
    refs[NY][...] = total.astype(BF16).T


def add_four(*parts):
    return call(
        add_kernel,
        far_out((BLOCK, D), BF16),
        1e3,
        grid=(2,),
        pins=(0,),
        in_specs=[pl.BlockSpec((HALF, BLOCK), lambda i: (i, 0))] * NY,
        out_specs=pl.BlockSpec((BLOCK, HALF), lambda i: (0, i)),
    )(*parts)


def after(values, *earlier):
    held = lax.optimization_barrier((tuple(values), earlier))
    return list(held[0])


def local(activations, cotangent, weight, feedback, q_previous):
    act, cot = activations[0], cotangent[0]
    old = feedback[0].reshape(2, HALF, COLS)
    place = jnp.stack([lax.axis_index("y"), lax.axis_index("c")]).astype(jnp.int32)

    q = q_previous.T
    t_send = t_rows(cot, q)
    t = exchange(t_send, MP)
    side = lambda value: ring(value, "c", NC, 1)
    act, cot_later, weight = after([act, cot, weight], t_send)
    fq, own0, own1 = f_rows(old, q, act)
    cot_side, weight_side = side(cot_later), side(weight)
    keep, p_send = p_rows(place, t, own0, own1, fq)
    p_send = pair_sum(keep, side(p_send)).reshape(16, 48, 128)

    mine, *rest = grad_parts(place, cot_later, cot_side, weight, weight_side)

    go0, go1 = after([own0, own1], t)
    low1, high0 = ring(go1, "y", NY, 1), ring(go0, "y", NY, 3)
    (p_plane,) = after([exchange(p_send, PLANE)], mine)
    p_sum = sum_spread(p_plane, NZ)
    go0, go1, far_go0, far_go1 = after([own0, own1, high0, low1], p_sum)
    low0, high1 = ring(go0, "y", NY, 1), ring(go1, "y", NY, 3)
    far0, far1 = ring(far_go0, "y", NY, 3), ring(far_go1, "y", NY, 1)

    p_z = exchange(p_sum, "z")
    p_half = sum_spread(p_z, 16)
    p = exchange(p_half, PLANE).reshape(PART, 128)
    later = after([low0, high0, far0, low1, high1, far1], p_half)

    own_sides = [side(value) for value in after([own0, own1], p_send)]
    sides = [side(value) for value in later]
    pairs = [(own0, own_sides[0]), *zip(later[:3], sides[:3])]
    pairs += [(own1, own_sides[1]), *zip(later[3:], sides[3:])]
    acts = [value for pair in pairs for value in pair]
    merged = merge(place, cot, old, acts)
    (p,) = after([p], merged)
    p_other = side(p)

    rest = after(rest, merged)
    parts = [ring(value, "y", NY, k) for k, value in zip((1, 2, 3), rest)]
    input_grad = add_four(mine, *parts)

    s_send = s_rows(place, p, merged, jnp.zeros((256, 128), F32), 0)
    s_send = s_rows(place, p_other, merged, s_send, 1)
    s = exchange(s_send.reshape(N_DP, 8, 128), DP)
    p, p_other = after([p, p_other], s_send)
    inverse = inverse_rows(p, p_other)
    (s,) = after([s], inverse)
    basis, packed = basis_rows(place, p, p_other, inverse)
    s = exchange(sum_spread(s, N_DP), DP).reshape(256, 128)
    (inverse,) = after([inverse], input_grad, basis)
    q_factor, feedback_new = last(s, inverse, packed, merged)
    return (
        input_grad[None],
        basis.T,
        q_factor.T,
        feedback_new.reshape(1, D, COLS),
    )


def solution(mesh):
    fine = Mesh(mesh.devices.reshape(NZ, NX, NY, NC), ("z", "x", "y", "c"))
    placed = (P(DP, MP, None), P(DP, None, MP), P(None, MP), P(DP, None, MP), P(MP, None))
    return jax.shard_map(
        local,
        mesh=fine,
        in_specs=placed,
        out_specs=(P(DP, MP, None), P(), P(MP, None), P(DP, None, MP)),
        check_vma=False,
    )
```

```python
import functools

import jax
import jax.numpy as jnp
from jax import lax
from jax.experimental import pallas as pl
from jax.experimental.pallas import tpu as pltpu
from jax.sharding import Mesh, PartitionSpec as P

F32 = jnp.float32
BF16 = jnp.bfloat16
NX, NY, NZ, NC = 4, 4, 8, 2
DP, MP, PLANE = ("z", "x"), ("y", "c"), ("x", "y")
N_DP = NZ * NX
HALF, COLS, RANK, BLOCK, D = 1536, 384, 64, 128, 3072
PART = HALF // 2
TILE = 512
STEPS = HALF // TILE
HIGHEST = lax.Precision.HIGHEST


def ring(value, axis, size, shift):
    return lax.ppermute(value, axis, [(i, (i + shift) % size) for i in range(size)])


def exchange(value, axes):
    return lax.all_to_all(value, axes, 0, 0, tiled=True)


def call(kernel, outs, flops, grid=None, pins=(), near=(), prefetch=False, **kwargs):
    if prefetch:
        names = ("in_specs", "out_specs", "scratch_shapes")
        spec = {name: kwargs.pop(name) for name in names if name in kwargs}
        kwargs["grid_spec"] = pltpu.PrefetchScalarGridSpec(
            num_scalar_prefetch=1, grid=grid, **spec
        )
        grid = None
    made = pl.pallas_call(
        kernel,
        out_shape=outs,
        compiler_params=pltpu.CompilerParams(vmem_limit_bytes=16 * 2**20),
        cost_estimate=pl.CostEstimate(
            flops=int(flops), bytes_accessed=1000, transcendentals=0
        ),
        **({} if grid is None else {"grid": grid}),
        **kwargs,
    )
    held = pltpu.with_memory_space_constraint
    where = {n: pltpu.HBM for n in pins} | {n: pltpu.VMEM for n in near}
    return lambda *args: made(
        *(held(v, where[n]) if n in where else v for n, v in enumerate(args))
    )


def out(shape, dtype=F32):
    return jax.ShapeDtypeStruct(shape, dtype)


def far_out(shape, dtype=F32):
    return pltpu.HBM(shape, dtype)


def dot(a, b, dims=((1,), (0,)), precision=None):
    return lax.dot_general(a, b, (dims, ((), ())), precision=precision, preferred_element_type=F32)


def two(value):
    high = value.astype(BF16)
    return high, (value - high.astype(F32)).astype(BF16)


def lanes(shape):
    return lax.broadcasted_iota(jnp.int32, shape, 1)


def sides(q):
    zero = jnp.zeros_like(q)
    return jnp.concatenate([q, zero], axis=0), jnp.concatenate([zero, q], axis=0)


ROWS = ((1,), (1,))


def t_kernel(cot_ref, q_ref, out_ref):
    left, right = sides(q_ref[...].astype(BF16))
    cot = cot_ref[...].reshape(4, 2, 64, COLS)
    first, second = cot[:, 0].reshape(256, COLS), cot[:, 1].reshape(256, COLS)
    both = dot(first, left, ROWS) + dot(second, right, ROWS)
    out_ref[...] = both.reshape(4, 64, 128)


def t_rows(cot, q):
    return call(
        t_kernel,
        out((8, 64, 128)),
        1e3,
        grid=(2,),
        pins=(0, 1),
        in_specs=[
            pl.BlockSpec((512, COLS), lambda i: (i, 0)),
            pl.BlockSpec((RANK, COLS), lambda i: (0, 0)),
        ],
        out_specs=pl.BlockSpec((4, 64, 128), lambda i: (i, 0, 0)),
    )(cot, q)


def f_kernel(old_ref, q_ref, first_ref, second_ref, fq_ref, act0_ref, act1_ref):
    left, right = sides(q_ref[...].astype(BF16))
    fq_ref[...] = dot(old_ref[0], left, ROWS) + dot(old_ref[1], right, ROWS)
    act0_ref[...] = first_ref[...].T
    act1_ref[...] = second_ref[...].T


def f_rows(old, q, act):
    return call(
        f_kernel,
        [far_out((HALF, 128))] + [out((HALF, BLOCK), BF16)] * 2,
        1e3,
        grid=(STEPS,),
        pins=(0, 1, 2, 3),
        in_specs=[
            pl.BlockSpec((2, TILE, COLS), lambda i: (0, i, 0)),
            pl.BlockSpec((RANK, COLS), lambda i: (0, 0)),
            pl.BlockSpec((BLOCK, TILE), lambda i: (0, i)),
            pl.BlockSpec((BLOCK, TILE), lambda i: (0, i + STEPS)),
        ],
        out_specs=[
            pl.BlockSpec((TILE, 128), lambda i: (i, 0)),
            pl.BlockSpec((TILE, BLOCK), lambda i: (i, 0)),
            pl.BlockSpec((TILE, BLOCK), lambda i: (i, 0)),
        ],
    )(old, q, act, act)


def p_kernel(place_ref, t_ref, act0_ref, act1_ref, fq_ref, keep_ref, send_ref):
    t = jnp.sum(t_ref[...], axis=0)
    low_lane = lanes(t.shape) < 64
    turned = pltpu.roll(t, 64, 1)
    rhs = jnp.concatenate(
        [
            jnp.where(low_lane, t, 0.0),
            jnp.where(low_lane, turned, 0.0),
            jnp.where(low_lane, 0.0, turned),
            jnp.where(low_lane, 0.0, t),
        ],
        axis=0,
    )
    lhs = jnp.concatenate([act0_ref[...], act1_ref[...]], axis=1)
    both = dot(lhs, jnp.concatenate(two(rhs), axis=1))
    total = both[:, :128] + both[:, 128:] + fq_ref[...]
    for n, ref in enumerate((keep_ref, send_ref)):

        @pl.when(pl.program_id(0) == n)
        def _():
            ref[...] = total


def half_of(i, place):
    return lax.rem(place[1] + i, 2)


def p_rows(place, t, act0, act1, fq):
    return call(
        p_kernel,
        [out((PART, 128))] * 2,
        1e3,
        grid=(2,),
        pins=(4,),
        prefetch=True,
        in_specs=[
            pl.BlockSpec((8, 64, 128), lambda i, place: (0, 0, 0)),
            pl.BlockSpec((PART, BLOCK), lambda i, place: (half_of(i, place), 0)),
            pl.BlockSpec((PART, BLOCK), lambda i, place: (half_of(i, place), 0)),
            pl.BlockSpec((PART, 128), lambda i, place: (half_of(i, place), 0)),
        ],
        out_specs=[pl.BlockSpec((PART, 128), lambda i, place: (0, 0))] * 2,
    )(place, t, act0, act1, fq)


def pair_kernel(a_ref, b_ref, out_ref):
    out_ref[...] = a_ref[...] + b_ref[...]


def pair_sum(a, b):
    return call(pair_kernel, far_out(a.shape), 1e3)(a, b)


def sum_kernel(in_ref, out_ref):
    total = jnp.sum(in_ref[...].astype(F32), axis=0)
    out_ref[...] = jnp.broadcast_to(total[None], out_ref.shape)


def sum_spread(value, count):
    return call(sum_kernel, out((count,) + value.shape[1:]), 1e3)(value)


def merge_kernel(place_ref, cot_ref, old_ref, *refs):
    acts, (out_ref, cot_rel) = refs[:-2], refs[-2:]
    y, c = place_ref[0], place_ref[1]

    @pl.when(pl.program_id(0) == 0)
    def _():
        for n, k in enumerate((0, 3, 1, 2)):
            for m in range(2):
                block = lax.rem(y + k, NY) * 2 + (c if m == 0 else 1 - c)
                cot_rel[pl.ds((2 * n + m) * BLOCK, BLOCK), :] = cot_ref[
                    pl.ds(pl.multiple_of(block * BLOCK, BLOCK), BLOCK), :
                ]

    for h in range(2):
        rows = jnp.concatenate([ref[...] for ref in acts[8 * h : 8 * h + 8]], axis=1)
        gradient = dot(rows, cot_rel[...])
        out_ref[h] = (gradient + old_ref[h].astype(F32)).astype(BF16)


def merge(place, cot, old, acts):
    return call(
        merge_kernel,
        pltpu.VMEM((2, HALF, COLS), BF16),
        1.5e10,
        grid=(STEPS,),
        pins=tuple(range(1, 19)),
        in_specs=[
            pl.BlockSpec(memory_space=pltpu.SMEM),
            pl.BlockSpec(cot.shape, lambda i: (0, 0)),
            pl.BlockSpec((2, TILE, COLS), lambda i: (0, i, 0)),
        ]
        + [pl.BlockSpec((TILE, BLOCK), lambda i: (i, 0))] * 16,
        out_specs=pl.BlockSpec((2, TILE, COLS), lambda i: (0, i, 0)),
        scratch_shapes=[pltpu.VMEM((8 * BLOCK, COLS), BF16)],
    )(place, cot, old, *acts)


def s_kernel(place_ref, p_ref, merged_ref, before_ref, out_ref):
    p = jnp.concatenate(two(p_ref[...]), axis=1)
    first = dot(p, merged_ref[0], ((0,), (0,)))
    second = dot(p, merged_ref[1], ((0,), (0,)))
    s = first[:64] + first[128:192] + second[64:128] + second[192:]
    for n in range(3):
        at = pl.ds(64 * n, 64)
        out_ref[at, :] = before_ref[at, :] + s[:, 128 * n : 128 * n + 128]
    out_ref[pl.ds(192, 64), :] = before_ref[pl.ds(192, 64), :]


def s_rows(place, p, merged, before, flip):
    return call(
        s_kernel,
        out((256, 128)),
        1e3,
        grid=(1,),
        near=(2,),
        prefetch=True,
        in_specs=[
            pl.BlockSpec((PART, 128), lambda i, place: (0, 0)),
            pl.BlockSpec((2, PART, COLS), lambda i, place: (0, half_of(flip, place), 0)),
            pl.BlockSpec((256, 128), lambda i, place: (0, 0)),
        ],
        out_specs=pl.BlockSpec((256, 128), lambda i, place: (0, 0)),
    )(place, p, merged, before)


def gram_half(p):
    high, rest = p.astype(BF16), p - p.astype(BF16).astype(F32)
    split = jnp.concatenate([high, *two(rest)], axis=1)
    blocks = dot(split, split, ((0,), (0,)))
    part = lambda a, b: blocks[128 * a : 128 * a + 128, 128 * b : 128 * b + 128]
    small = part(0, 2) + part(2, 0) + part(1, 1)
    return part(0, 0) + (part(0, 1) + part(1, 0) + small)


def inverse_kernel(own_ref, other_ref, inverse_ref):
    pair = gram_half(own_ref[...]) + gram_half(other_ref[...])
    gram = pair[:64, :64] + pair[64:, 64:]
    row = lax.broadcasted_iota(jnp.int32, (64, 64), 0)
    unit = jnp.where(row == lanes((64, 64)), 1.0, 0.0)
    table = jnp.concatenate([gram, unit], axis=1)
    tiles = [table[8 * i : 8 * i + 8] for i in range(8)]
    sub = lax.broadcasted_iota(jnp.int32, (8, 128), 0)
    for j in range(0, 64, 4):
        at, inner = j // 8, j % 8
        columns = [
            {i: jnp.broadcast_to(tiles[i][:, j + k : j + k + 1], (8, 128)) for i in range(at, 8)}
            for k in range(4)
        ]
        for k in range(4):
            n = inner + k
            scale = 1.0 / columns[k][at][n : n + 1]
            heads = [columns[m][at][n : n + 1] for m in range(k + 1, 4)]
            pivot = tiles[at][n : n + 1]
            for i in range(at, 8):
                factor = columns[k][i] * scale
                if i == at:
                    factor = jnp.where(sub > n, factor, 0.0)
                for m, head in zip(range(k + 1, 4), heads):
                    columns[m][i] = columns[m][i] - factor * head
                tiles[i] = tiles[i] - factor * pivot
    table = jnp.concatenate(tiles, axis=0)
    lane = lanes((64, 128))
    here = lax.broadcasted_iota(jnp.int32, (64, 128), 0) == lane
    diagonal = jnp.sum(jnp.where(here, table, 0.0), axis=1, keepdims=True)
    right = jnp.where(lane >= 64, table, 0.0) / jnp.sqrt(diagonal)
    inverse_ref[...] = jnp.concatenate([pltpu.roll(right, 64, 1), right], axis=0)


def basis_kernel(place_ref, own_ref, other_ref, inverse_ref, basis_ref, packed_ref):
    inverse = inverse_ref[...]
    for n, ref in enumerate((own_ref, other_ref)):
        half = lax.rem(place_ref[1] + n, 2)
        start = pl.multiple_of(half * PART, PART)
        p = ref[...]
        packed_ref[pl.ds(start, PART), :] = dot(p, inverse, ROWS, HIGHEST)
        turned = dot(inverse, p, ROWS, HIGHEST)
        for h in range(2):
            at = pl.ds(pl.multiple_of(start + h * HALF, PART), PART)
            basis_ref[:, at] = turned[64 * h : 64 * h + 64]


def inverse_rows(own, other):
    return call(inverse_kernel, out((128, 128)), 1e3)(own, other)


def basis_rows(place, own, other, inverse):
    return call(
        basis_kernel,
        [far_out((RANK, D)), out((HALF, 128))],
        1e3,
        in_specs=[pl.BlockSpec(memory_space=pltpu.SMEM)] + [pl.BlockSpec()] * 3,
    )(place, own, other, inverse)


def last_kernel(s_ref, inverse_ref, packed_ref, merged_ref, q_ref, new_ref, rhs):
    @pl.when(pl.program_id(0) == 0)
    def _():
        s = jnp.concatenate([s_ref[pl.ds(64 * n, 64), :] for n in range(3)], axis=1)
        q = dot(inverse_ref[0:64, 0:64], s, precision=HIGHEST) * (1.0 / N_DP)
        q_ref[...] = q
        high, low = two(q)
        zero = jnp.zeros_like(high)
        for h in range(2):
            pair = lambda v: [zero, v] if h else [v, zero]
            rhs[h] = jnp.concatenate(pair(high) + pair(high) + pair(low), axis=0)

    high, low = two(packed_ref[...])
    lhs = jnp.concatenate([high, low, high], axis=1)
    for h in range(2):
        new_ref[h] = (merged_ref[h].astype(F32) - dot(lhs, rhs[h])).astype(BF16)


def last(s, inverse, packed, merged):
    return call(
        last_kernel,
        [far_out((RANK, COLS)), far_out((2, HALF, COLS), BF16)],
        1e3,
        grid=(STEPS,),
        near=(3,),
        in_specs=[
            pl.BlockSpec((256, 128), lambda i: (0, 0)),
            pl.BlockSpec((128, 128), lambda i: (0, 0)),
            pl.BlockSpec((TILE, 128), lambda i: (i, 0)),
            pl.BlockSpec((2, TILE, COLS), lambda i: (0, i, 0)),
        ],
        out_specs=[
            pl.BlockSpec((RANK, COLS), lambda i: (0, 0)),
            pl.BlockSpec((2, TILE, COLS), lambda i: (0, i, 0)),
        ],
        scratch_shapes=[pltpu.VMEM((2, 384, COLS), BF16)],
    )(s, inverse, packed, merged)


def grad_kernel(half, place_ref, cot_ref, weight_ref, cot_side_ref, weight_side_ref, *refs):
    out_refs, rows = refs[-1 - NY : -1], refs[-1]

    @pl.when(pl.program_id(0) == 0)
    def _():
        for k in range(NY):
            block = lax.rem(place_ref[0] + k, NY) * 2 + place_ref[1]
            start = pl.multiple_of(block * BLOCK, BLOCK)
            for n, ref in enumerate((cot_ref, cot_side_ref)):
                rows[n * COLS : (n + 1) * COLS, k * BLOCK : (k + 1) * BLOCK] = ref[
                    pl.ds(start, BLOCK), :
                ].T

    weight = jnp.concatenate([weight_ref[...], weight_side_ref[...]], axis=1)
    part = dot(weight, rows[...]).astype(BF16)
    mine, up, far, down = (part[:, k * BLOCK : (k + 1) * BLOCK] for k in range(NY))
    joined = (far, down, up) if half == 0 else (up, far, down)
    for ref, value in zip(out_refs, (mine, *joined)):
        ref[...] = value


def grad_parts(place, cot, cot_side, weight, weight_side, half, before=()):
    whole = pl.BlockSpec(cot.shape, lambda i: (0, 0))
    tile = pl.BlockSpec((PART, COLS), lambda i: (i + half * 2, 0))
    return call(
        functools.partial(grad_kernel, half),
        [far_out((D, BLOCK), BF16)] * 3 + [far_out((HALF, BLOCK), BF16)],
        1e3,
        grid=(2,),
        pins=(1, 3) + tuple(range(5, 5 + len(before))),
        in_specs=[pl.BlockSpec(memory_space=pltpu.SMEM), whole, tile, whole, tile]
        + [pl.BlockSpec(memory_space=pl.ANY)] * len(before),
        out_specs=[pl.BlockSpec((PART, BLOCK), lambda i: (i + half * 2, 0))] * 3
        + [pl.BlockSpec((PART, BLOCK), lambda i: (i, 0))],
        scratch_shapes=[pltpu.VMEM((2 * COLS, NY * BLOCK), BF16)],
        input_output_aliases={5 + n: n for n in range(len(before))},
    )(place, cot, weight, cot_side, weight_side, *before)


def join_kernel(a_ref, b_ref, c_ref, d_ref, up_ref, down_ref):
    up_ref[...] = (a_ref[...].astype(F32) + b_ref[...].astype(F32)).astype(BF16)
    down_ref[...] = (c_ref[...].astype(F32) + d_ref[...].astype(F32)).astype(BF16)


def join(up, got_plus, down, got_minus):
    first = pl.BlockSpec((HALF, BLOCK), lambda i: (0, 0))
    second = pl.BlockSpec((HALF, BLOCK), lambda i: (1, 0))
    return call(
        join_kernel,
        [far_out((HALF, BLOCK), BF16)] * 2,
        1e3,
        grid=(1,),
        pins=(0, 2),
        in_specs=[first, first, first, second],
        out_specs=[first, first],
    )(up, got_plus, down, got_minus)


def add_kernel(mine_ref, plus_ref, minus_ref, up_ref, down_ref, out_ref):
    step = pl.program_id(0)

    def store(*refs):
        total = refs[0][...].astype(F32)
        for ref in refs[1:]:
            total += ref[...].astype(F32)
        out_ref[...] = total.astype(BF16).T

    pl.when(step == 0)(lambda: store(mine_ref, minus_ref, up_ref))
    pl.when(step == 1)(lambda: store(mine_ref, plus_ref, down_ref))


def add_three(mine, got_plus, got_minus, got_up, got_down):
    first = pl.BlockSpec((HALF, BLOCK), lambda i: (0, 0))
    second = pl.BlockSpec((HALF, BLOCK), lambda i: (1, 0))
    return call(
        add_kernel,
        far_out((BLOCK, D), BF16),
        1e3,
        grid=(2,),
        pins=(0,),
        in_specs=[pl.BlockSpec((HALF, BLOCK), lambda i: (i, 0)), second, first, first, first],
        out_specs=pl.BlockSpec((BLOCK, HALF), lambda i: (0, i)),
    )(mine, got_plus, got_minus, got_up, got_down)


def after(values, *earlier):
    held = lax.optimization_barrier((tuple(values), earlier))
    return list(held[0])


def local(activations, cotangent, weight, feedback, q_previous):
    act, cot = activations[0], cotangent[0]
    old = feedback[0].reshape(2, HALF, COLS)
    place = jnp.stack([lax.axis_index("y"), lax.axis_index("c")]).astype(jnp.int32)

    q = q_previous.T
    t_send = t_rows(cot, q)
    t = exchange(t_send, MP)
    side = lambda value: ring(value, "c", NC, 1)
    act, cot_later, weight = after([act, cot, weight], t_send)
    fq, own0, own1 = f_rows(old, q, act)
    cot_side, weight_side = side(cot_later), side(weight)
    keep, p_send = p_rows(place, t, own0, own1, fq)
    p_send = pair_sum(keep, side(p_send)).reshape(16, 48, 128)

    inputs = (place, cot_later, cot_side, weight, weight_side)
    *first, up = grad_parts(*inputs, 0)
    mine = first[0]

    go0, go1 = after([own0, own1], t)
    low1, high0 = ring(go1, "y", NY, 1), ring(go0, "y", NY, 3)
    (p_plane,) = after([exchange(p_send, PLANE)], mine)
    p_sum = sum_spread(p_plane, NZ)
    low0, high1 = ring(go0, "y", NY, 1), ring(go1, "y", NY, 3)
    far_go0, far_go1 = after([high0, low1], p_sum)
    far0, far1 = ring(far_go0, "y", NY, 3), ring(far_go1, "y", NY, 1)

    p_z = exchange(p_sum, "z")
    first = after(first, p_sum)
    mine, plus, minus, down = grad_parts(*inputs, 1, first)
    (p_z,) = after([p_z], mine)
    p_half = sum_spread(p_z, 16)
    p = exchange(p_half, PLANE).reshape(PART, 128)
    later = after([low0, high0, far0, low1, high1, far1], p_half)

    own_sides = [side(value) for value in after([own0, own1], p_send)]
    sides = [side(value) for value in later]
    pairs = [(own0, own_sides[0]), *zip(later[:3], sides[:3])]
    pairs += [(own1, own_sides[1]), *zip(later[3:], sides[3:])]
    acts = [value for pair in pairs for value in pair]
    merged = merge(place, cot, old, acts)
    (p,) = after([p], merged)
    p_other = side(p)

    plus, minus = after([plus, minus], merged)
    got_plus, got_minus = ring(plus, "y", NY, 1), ring(minus, "y", NY, 3)

    s_send = s_rows(place, p, merged, jnp.zeros((256, 128), F32), 0)
    s_send = s_rows(place, p_other, merged, s_send, 1)
    s = exchange(s_send.reshape(N_DP, 8, 128), DP)
    p, p_other = after([p, p_other], s_send)
    inverse = inverse_rows(p, p_other)
    (up,) = after([up], inverse)
    up, down = join(up, got_plus, down, got_minus)
    (s,) = after([s], inverse, up)
    got_up, got_down = ring(up, "y", NY, 1), ring(down, "y", NY, 3)
    input_grad = add_three(mine, got_plus, got_minus, got_up, got_down)
    basis, packed = basis_rows(place, p, p_other, inverse)
    s = exchange(sum_spread(s, N_DP), DP).reshape(256, 128)
    (inverse,) = after([inverse], basis, input_grad)
    q_factor, feedback_new = last(s, inverse, packed, merged)
    return (
        input_grad[None],
        basis.T,
        q_factor.T,
        feedback_new.reshape(1, D, COLS),
    )


def solution(mesh):
    fine = Mesh(mesh.devices.reshape(NZ, NX, NY, NC), ("z", "x", "y", "c"))
    placed = (P(DP, MP, None), P(DP, None, MP), P(None, MP), P(DP, None, MP), P(MP, None))
    return jax.shard_map(
        local,
        mesh=fine,
        in_specs=placed,
        out_specs=(P(DP, MP, None), P(), P(MP, None), P(DP, None, MP)),
        check_vma=False,
    )
```

```python
import functools

import jax
import jax.numpy as jnp
from jax import lax
from jax.experimental import pallas as pl
from jax.experimental.pallas import tpu as pltpu
from jax.sharding import Mesh, PartitionSpec as P

F32 = jnp.float32
BF16 = jnp.bfloat16
NX, NY, NZ, NC = 4, 4, 8, 2
DP, MP, PLANE = ("z", "x"), ("y", "c"), ("x", "y")
N_DP = NZ * NX
BACK = list(range(N_DP))[::-1]
HALF, COLS, RANK, BLOCK, D = 1536, 384, 64, 128, 3072
PART = HALF // 2
TILE = 512
STEPS = HALF // TILE
HIGHEST = lax.Precision.HIGHEST


def ring(value, axis, size, shift):
    return lax.ppermute(value, axis, [(i, (i + shift) % size) for i in range(size)])


def exchange(value, axes, order=None):
    groups = None if order is None else [order]
    return lax.all_to_all(value, axes, 0, 0, axis_index_groups=groups, tiled=True)


def call(kernel, outs, flops, grid=None, pins=(), near=(), prefetch=False, **kwargs):
    if prefetch:
        names = ("in_specs", "out_specs", "scratch_shapes")
        spec = {name: kwargs.pop(name) for name in names if name in kwargs}
        kwargs["grid_spec"] = pltpu.PrefetchScalarGridSpec(
            num_scalar_prefetch=1, grid=grid, **spec
        )
        grid = None
    made = pl.pallas_call(
        kernel,
        out_shape=outs,
        compiler_params=pltpu.CompilerParams(vmem_limit_bytes=16 * 2**20),
        cost_estimate=pl.CostEstimate(
            flops=int(flops), bytes_accessed=1000, transcendentals=0
        ),
        **({} if grid is None else {"grid": grid}),
        **kwargs,
    )
    held = pltpu.with_memory_space_constraint
    where = {n: pltpu.HBM for n in pins} | {n: pltpu.VMEM for n in near}
    return lambda *args: made(
        *(held(v, where[n]) if n in where else v for n, v in enumerate(args))
    )


def out(shape, dtype=F32):
    return jax.ShapeDtypeStruct(shape, dtype)


def far_out(shape, dtype=F32):
    return pltpu.HBM(shape, dtype)


def dot(a, b, dims=((1,), (0,)), precision=None):
    return lax.dot_general(a, b, (dims, ((), ())), precision=precision, preferred_element_type=F32)


def two(value):
    high = value.astype(BF16)
    return high, (value - high.astype(F32)).astype(BF16)


def lanes(shape):
    return lax.broadcasted_iota(jnp.int32, shape, 1)


def sides(q):
    zero = jnp.zeros_like(q)
    return jnp.concatenate([q, zero], axis=0), jnp.concatenate([zero, q], axis=0)


ROWS = ((1,), (1,))


def t_kernel(cot_ref, q_ref, out_ref):
    left, right = sides(q_ref[...].astype(BF16))
    cot = cot_ref[...].reshape(4, 2, 64, COLS)
    first, second = cot[:, 0].reshape(256, COLS), cot[:, 1].reshape(256, COLS)
    both = dot(first, left, ROWS) + dot(second, right, ROWS)
    out_ref[...] = both.reshape(4, 64, 128)


def t_rows(cot, q):
    return call(
        t_kernel,
        out((8, 64, 128)),
        1e3,
        grid=(2,),
        pins=(0, 1),
        in_specs=[
            pl.BlockSpec((512, COLS), lambda i: (i, 0)),
            pl.BlockSpec((RANK, COLS), lambda i: (0, 0)),
        ],
        out_specs=pl.BlockSpec((4, 64, 128), lambda i: (i, 0, 0)),
    )(cot, q)


def f_kernel(old_ref, q_ref, first_ref, second_ref, fq_ref, act0_ref, act1_ref):
    left, right = sides(q_ref[...].astype(BF16))
    fq_ref[...] = dot(old_ref[0], left, ROWS) + dot(old_ref[1], right, ROWS)
    act0_ref[...] = first_ref[...].T
    act1_ref[...] = second_ref[...].T


def f_rows(old, q, act):
    return call(
        f_kernel,
        [far_out((HALF, 128))] + [out((HALF, BLOCK), BF16)] * 2,
        1e3,
        grid=(STEPS,),
        pins=(0, 1, 2, 3),
        in_specs=[
            pl.BlockSpec((2, TILE, COLS), lambda i: (0, i, 0)),
            pl.BlockSpec((RANK, COLS), lambda i: (0, 0)),
            pl.BlockSpec((BLOCK, TILE), lambda i: (0, i)),
            pl.BlockSpec((BLOCK, TILE), lambda i: (0, i + STEPS)),
        ],
        out_specs=[
            pl.BlockSpec((TILE, 128), lambda i: (i, 0)),
            pl.BlockSpec((TILE, BLOCK), lambda i: (i, 0)),
            pl.BlockSpec((TILE, BLOCK), lambda i: (i, 0)),
        ],
    )(old, q, act, act)


def p_kernel(place_ref, t_ref, act0_ref, act1_ref, fq_ref, keep_ref, send_ref):
    t = jnp.sum(t_ref[...], axis=0)
    low_lane = lanes(t.shape) < 64
    turned = pltpu.roll(t, 64, 1)
    rhs = jnp.concatenate(
        [
            jnp.where(low_lane, t, 0.0),
            jnp.where(low_lane, turned, 0.0),
            jnp.where(low_lane, 0.0, turned),
            jnp.where(low_lane, 0.0, t),
        ],
        axis=0,
    )
    lhs = jnp.concatenate([act0_ref[...], act1_ref[...]], axis=1)
    both = dot(lhs, jnp.concatenate(two(rhs), axis=1))
    total = both[:, :128] + both[:, 128:] + fq_ref[...]
    for n, ref in enumerate((keep_ref, send_ref)):

        @pl.when(pl.program_id(0) == n)
        def _():
            ref[...] = total


def half_of(i, place):
    return lax.rem(place[1] + i, 2)


def p_rows(place, t, act0, act1, fq):
    return call(
        p_kernel,
        [out((PART, 128))] * 2,
        1e3,
        grid=(2,),
        pins=(4,),
        prefetch=True,
        in_specs=[
            pl.BlockSpec((8, 64, 128), lambda i, place: (0, 0, 0)),
            pl.BlockSpec((PART, BLOCK), lambda i, place: (half_of(i, place), 0)),
            pl.BlockSpec((PART, BLOCK), lambda i, place: (half_of(i, place), 0)),
            pl.BlockSpec((PART, 128), lambda i, place: (half_of(i, place), 0)),
        ],
        out_specs=[pl.BlockSpec((PART, 128), lambda i, place: (0, 0))] * 2,
    )(place, t, act0, act1, fq)


def pair_kernel(a_ref, b_ref, out_ref):
    out_ref[...] = a_ref[...] + b_ref[...]


def pair_sum(a, b):
    return call(pair_kernel, far_out(a.shape), 1e3)(a, b)


def sum_kernel(in_ref, out_ref):
    total = jnp.sum(in_ref[...].astype(F32), axis=0)
    out_ref[...] = jnp.broadcast_to(total[None], out_ref.shape)


def sum_spread(value, count):
    return call(sum_kernel, out((count,) + value.shape[1:]), 1e3)(value)


def merge_kernel(place_ref, cot_ref, old_ref, *refs):
    acts, (out_ref, cot_rel) = refs[:-2], refs[-2:]
    y, c = place_ref[0], place_ref[1]

    @pl.when(pl.program_id(0) == 0)
    def _():
        for n, k in enumerate((0, 3, 1, 2)):
            for m in range(2):
                block = lax.rem(y + k, NY) * 2 + (c if m == 0 else 1 - c)
                cot_rel[pl.ds((2 * n + m) * BLOCK, BLOCK), :] = cot_ref[
                    pl.ds(pl.multiple_of(block * BLOCK, BLOCK), BLOCK), :
                ]

    for h in range(2):
        rows = jnp.concatenate([ref[...] for ref in acts[8 * h : 8 * h + 8]], axis=1)
        gradient = dot(rows, cot_rel[...])
        out_ref[h] = (gradient + old_ref[h].astype(F32)).astype(BF16)


def merge(place, cot, old, acts):
    return call(
        merge_kernel,
        pltpu.VMEM((2, HALF, COLS), BF16),
        1.5e10,
        grid=(STEPS,),
        pins=tuple(range(1, 19)),
        in_specs=[
            pl.BlockSpec(memory_space=pltpu.SMEM),
            pl.BlockSpec(cot.shape, lambda i: (0, 0)),
            pl.BlockSpec((2, TILE, COLS), lambda i: (0, i, 0)),
        ]
        + [pl.BlockSpec((TILE, BLOCK), lambda i: (i, 0))] * 16,
        out_specs=pl.BlockSpec((2, TILE, COLS), lambda i: (0, i, 0)),
        scratch_shapes=[pltpu.VMEM((8 * BLOCK, COLS), BF16)],
    )(place, cot, old, *acts)


def s_kernel(place_ref, p_ref, merged_ref, before_ref, out_ref):
    p = jnp.concatenate(two(p_ref[...]), axis=1)
    first = dot(p, merged_ref[0], ((0,), (0,)))
    second = dot(p, merged_ref[1], ((0,), (0,)))
    s = first[:64] + first[128:192] + second[64:128] + second[192:]
    for n in range(3):
        at = pl.ds(64 * n, 64)
        out_ref[at, :] = before_ref[at, :] + s[:, 128 * n : 128 * n + 128]
    out_ref[pl.ds(192, 64), :] = before_ref[pl.ds(192, 64), :]


def s_rows(place, p, merged, before, flip):
    return call(
        s_kernel,
        out((256, 128)),
        1e3,
        grid=(1,),
        near=(2,),
        prefetch=True,
        in_specs=[
            pl.BlockSpec((PART, 128), lambda i, place: (0, 0)),
            pl.BlockSpec((2, PART, COLS), lambda i, place: (0, half_of(flip, place), 0)),
            pl.BlockSpec((256, 128), lambda i, place: (0, 0)),
        ],
        out_specs=pl.BlockSpec((256, 128), lambda i, place: (0, 0)),
    )(place, p, merged, before)


def gram_half(p):
    high, rest = p.astype(BF16), p - p.astype(BF16).astype(F32)
    split = jnp.concatenate([high, *two(rest)], axis=1)
    blocks = dot(split, split, ((0,), (0,)))
    part = lambda a, b: blocks[128 * a : 128 * a + 128, 128 * b : 128 * b + 128]
    small = part(0, 2) + part(2, 0) + part(1, 1)
    return part(0, 0) + (part(0, 1) + part(1, 0) + small)


def inverse_kernel(own_ref, other_ref, inverse_ref):
    pair = gram_half(own_ref[...]) + gram_half(other_ref[...])
    gram = pair[:64, :64] + pair[64:, 64:]
    row = lax.broadcasted_iota(jnp.int32, (64, 64), 0)
    unit = jnp.where(row == lanes((64, 64)), 1.0, 0.0)
    table = jnp.concatenate([gram, unit], axis=1)
    tiles = [table[8 * i : 8 * i + 8] for i in range(8)]
    sub = lax.broadcasted_iota(jnp.int32, (8, 128), 0)
    for j in range(0, 64, 4):
        at, inner = j // 8, j % 8
        columns = [
            {i: jnp.broadcast_to(tiles[i][:, j + k : j + k + 1], (8, 128)) for i in range(at, 8)}
            for k in range(4)
        ]
        for k in range(4):
            n = inner + k
            scale = 1.0 / columns[k][at][n : n + 1]
            heads = [columns[m][at][n : n + 1] for m in range(k + 1, 4)]
            pivot = tiles[at][n : n + 1]
            for i in range(at, 8):
                factor = columns[k][i] * scale
                if i == at:
                    factor = jnp.where(sub > n, factor, 0.0)
                for m, head in zip(range(k + 1, 4), heads):
                    columns[m][i] = columns[m][i] - factor * head
                tiles[i] = tiles[i] - factor * pivot
    table = jnp.concatenate(tiles, axis=0)
    lane = lanes((64, 128))
    here = lax.broadcasted_iota(jnp.int32, (64, 128), 0) == lane
    diagonal = jnp.sum(jnp.where(here, table, 0.0), axis=1, keepdims=True)
    right = jnp.where(lane >= 64, table, 0.0) / jnp.sqrt(diagonal)
    inverse_ref[...] = jnp.concatenate([pltpu.roll(right, 64, 1), right], axis=0)


def basis_kernel(place_ref, own_ref, other_ref, inverse_ref, basis_ref, packed_ref):
    inverse = inverse_ref[...]
    for n, ref in enumerate((own_ref, other_ref)):
        half = lax.rem(place_ref[1] + n, 2)
        start = pl.multiple_of(half * PART, PART)
        p = ref[...]
        packed_ref[pl.ds(start, PART), :] = dot(p, inverse, ROWS, HIGHEST)
        turned = dot(inverse, p, ROWS, HIGHEST)
        for h in range(2):
            at = pl.ds(pl.multiple_of(start + h * HALF, PART), PART)
            basis_ref[:, at] = turned[64 * h : 64 * h + 64]


def inverse_rows(own, other):
    return call(inverse_kernel, out((128, 128)), 1e3)(own, other)


def basis_rows(place, own, other, inverse):
    return call(
        basis_kernel,
        [far_out((RANK, D)), out((HALF, 128))],
        1e3,
        in_specs=[pl.BlockSpec(memory_space=pltpu.SMEM)] + [pl.BlockSpec()] * 3,
    )(place, own, other, inverse)


def last_kernel(s_ref, inverse_ref, packed_ref, merged_ref, q_ref, new_ref, rhs):
    @pl.when(pl.program_id(0) == 0)
    def _():
        s = jnp.concatenate([s_ref[pl.ds(64 * n, 64), :] for n in range(3)], axis=1)
        q = dot(inverse_ref[0:64, 0:64], s, precision=HIGHEST) * (1.0 / N_DP)
        q_ref[...] = q
        high, low = two(q)
        zero = jnp.zeros_like(high)
        for h in range(2):
            pair = lambda v: [zero, v] if h else [v, zero]
            rhs[h] = jnp.concatenate(pair(high) + pair(high) + pair(low), axis=0)

    high, low = two(packed_ref[...])
    lhs = jnp.concatenate([high, low, high], axis=1)
    for h in range(2):
        new_ref[h] = (merged_ref[h].astype(F32) - dot(lhs, rhs[h])).astype(BF16)


def last(s, inverse, packed, merged):
    return call(
        last_kernel,
        [far_out((RANK, COLS)), far_out((2, HALF, COLS), BF16)],
        1e3,
        grid=(STEPS,),
        near=(3,),
        in_specs=[
            pl.BlockSpec((256, 128), lambda i: (0, 0)),
            pl.BlockSpec((128, 128), lambda i: (0, 0)),
            pl.BlockSpec((TILE, 128), lambda i: (i, 0)),
            pl.BlockSpec((2, TILE, COLS), lambda i: (0, i, 0)),
        ],
        out_specs=[
            pl.BlockSpec((RANK, COLS), lambda i: (0, 0)),
            pl.BlockSpec((2, TILE, COLS), lambda i: (0, i, 0)),
        ],
        scratch_shapes=[pltpu.VMEM((2, 384, COLS), BF16)],
    )(s, inverse, packed, merged)


def grad_kernel(half, place_ref, cot_ref, weight_ref, cot_side_ref, weight_side_ref, *refs):
    out_refs, rows = refs[-1 - NY : -1], refs[-1]

    @pl.when(pl.program_id(0) == 0)
    def _():
        for k in range(NY):
            block = lax.rem(place_ref[0] + k, NY) * 2 + place_ref[1]
            start = pl.multiple_of(block * BLOCK, BLOCK)
            for n, ref in enumerate((cot_ref, cot_side_ref)):
                rows[n * COLS : (n + 1) * COLS, k * BLOCK : (k + 1) * BLOCK] = ref[
                    pl.ds(start, BLOCK), :
                ].T

    weight = jnp.concatenate([weight_ref[...], weight_side_ref[...]], axis=1)
    part = dot(weight, rows[...]).astype(BF16)
    mine, up, far, down = (part[:, k * BLOCK : (k + 1) * BLOCK] for k in range(NY))
    joined = (far, down, up) if half == 0 else (up, far, down)
    for ref, value in zip(out_refs, (mine, *joined)):
        ref[...] = value


def grad_parts(place, cot, cot_side, weight, weight_side, half, before=()):
    whole = pl.BlockSpec(cot.shape, lambda i: (0, 0))
    tile = pl.BlockSpec((PART, COLS), lambda i: (i + half * 2, 0))
    return call(
        functools.partial(grad_kernel, half),
        [far_out((D, BLOCK), BF16)] * 3 + [far_out((HALF, BLOCK), BF16)],
        1e3,
        grid=(2,),
        pins=(1, 3) + tuple(range(5, 5 + len(before))),
        in_specs=[pl.BlockSpec(memory_space=pltpu.SMEM), whole, tile, whole, tile]
        + [pl.BlockSpec(memory_space=pl.ANY)] * len(before),
        out_specs=[pl.BlockSpec((PART, BLOCK), lambda i: (i + half * 2, 0))] * 3
        + [pl.BlockSpec((PART, BLOCK), lambda i: (i, 0))],
        scratch_shapes=[pltpu.VMEM((2 * COLS, NY * BLOCK), BF16)],
        input_output_aliases={5 + n: n for n in range(len(before))},
    )(place, cot, weight, cot_side, weight_side, *before)


def join_kernel(a_ref, b_ref, c_ref, d_ref, up_ref, down_ref):
    up_ref[...] = (a_ref[...].astype(F32) + b_ref[...].astype(F32)).astype(BF16)
    down_ref[...] = (c_ref[...].astype(F32) + d_ref[...].astype(F32)).astype(BF16)


def join(up, got_plus, down, got_minus):
    first = pl.BlockSpec((HALF, BLOCK), lambda i: (0, 0))
    second = pl.BlockSpec((HALF, BLOCK), lambda i: (1, 0))
    return call(
        join_kernel,
        [far_out((HALF, BLOCK), BF16)] * 2,
        1e3,
        grid=(1,),
        pins=(0, 2),
        in_specs=[first, first, first, second],
        out_specs=[first, first],
    )(up, got_plus, down, got_minus)


def add_kernel(mine_ref, plus_ref, minus_ref, up_ref, down_ref, out_ref):
    step = pl.program_id(0)

    def store(*refs):
        total = refs[0][...].astype(F32)
        for ref in refs[1:]:
            total += ref[...].astype(F32)
        out_ref[...] = total.astype(BF16).T

    pl.when(step == 0)(lambda: store(mine_ref, minus_ref, up_ref))
    pl.when(step == 1)(lambda: store(mine_ref, plus_ref, down_ref))


def add_three(mine, got_plus, got_minus, got_up, got_down):
    first = pl.BlockSpec((HALF, BLOCK), lambda i: (0, 0))
    second = pl.BlockSpec((HALF, BLOCK), lambda i: (1, 0))
    return call(
        add_kernel,
        far_out((BLOCK, D), BF16),
        1e3,
        grid=(2,),
        pins=(0,),
        in_specs=[pl.BlockSpec((HALF, BLOCK), lambda i: (i, 0)), second, first, first, first],
        out_specs=pl.BlockSpec((BLOCK, HALF), lambda i: (0, i)),
    )(mine, got_plus, got_minus, got_up, got_down)


def after(values, *earlier):
    held = lax.optimization_barrier((tuple(values), earlier))
    return list(held[0])


def local(activations, cotangent, weight, feedback, q_previous):
    act, cot = activations[0], cotangent[0]
    old = feedback[0].reshape(2, HALF, COLS)
    place = jnp.stack([lax.axis_index("y"), lax.axis_index("c")]).astype(jnp.int32)

    q = q_previous.T
    t_send = t_rows(cot, q)
    t = exchange(t_send, MP)
    side = lambda value: ring(value, "c", NC, 1)
    act, cot_later, weight = after([act, cot, weight], t_send)
    fq, own0, own1 = f_rows(old, q, act)
    cot_side, weight_side = side(cot_later), side(weight)
    keep, p_send = p_rows(place, t, own0, own1, fq)
    p_send = pair_sum(keep, side(p_send)).reshape(16, 48, 128)

    inputs = (place, cot_later, cot_side, weight, weight_side)
    *first, up = grad_parts(*inputs, 0)
    mine = first[0]

    go0, go1 = after([own0, own1], t)
    low1, high0 = ring(go1, "y", NY, 1), ring(go0, "y", NY, 3)
    (p_plane,) = after([exchange(p_send, PLANE)], mine)
    p_sum = sum_spread(p_plane, NZ)
    low0, high1 = ring(go0, "y", NY, 1), ring(go1, "y", NY, 3)
    far_go0, far_go1 = after([high0, low1], p_sum)
    far0, far1 = ring(far_go0, "y", NY, 3), ring(far_go1, "y", NY, 1)

    p_z = exchange(p_sum, "z")
    first = after(first, p_sum)
    mine, plus, minus, down = grad_parts(*inputs, 1, first)
    (p_z,) = after([p_z], mine)
    p_half = sum_spread(p_z, 16)
    p = exchange(p_half, PLANE).reshape(PART, 128)
    later = after([low0, high0, far0, low1, high1, far1], p_half)

    own_sides = [side(value) for value in after([own0, own1], p_send)]
    sides = [side(value) for value in later]
    pairs = [(own0, own_sides[0]), *zip(later[:3], sides[:3])]
    pairs += [(own1, own_sides[1]), *zip(later[3:], sides[3:])]
    acts = [value for pair in pairs for value in pair]
    merged = merge(place, cot, old, acts)
    (p,) = after([p], merged)
    p_other = side(p)

    plus, minus = after([plus, minus], *sides)
    got_plus, got_minus = ring(plus, "y", NY, 1), ring(minus, "y", NY, 3)

    s_send = s_rows(place, p, merged, jnp.zeros((256, 128), F32), 0)
    s_send = s_rows(place, p_other, merged, s_send, 1)
    s = exchange(s_send.reshape(N_DP, 8, 128), DP, BACK)
    p, p_other = after([p, p_other], s_send)
    inverse = inverse_rows(p, p_other)
    (up,) = after([up], inverse)
    up, down = join(up, got_plus, down, got_minus)
    (s,) = after([s], inverse, up)
    got_up, got_down = ring(up, "y", NY, 1), ring(down, "y", NY, 3)
    input_grad = add_three(mine, got_plus, got_minus, got_up, got_down)
    basis, packed = basis_rows(place, p, p_other, inverse)
    s = exchange(sum_spread(s, N_DP), DP, BACK).reshape(256, 128)
    (inverse,) = after([inverse], basis, input_grad)
    q_factor, feedback_new = last(s, inverse, packed, merged)
    return (
        input_grad[None],
        basis.T,
        q_factor.T,
        feedback_new.reshape(1, D, COLS),
    )


def solution(mesh):
    fine = Mesh(mesh.devices.reshape(NZ, NX, NY, NC), ("z", "x", "y", "c"))
    placed = (P(DP, MP, None), P(DP, None, MP), P(None, MP), P(DP, None, MP), P(MP, None))
    return jax.shard_map(
        local,
        mesh=fine,
        in_specs=placed,
        out_specs=(P(DP, MP, None), P(), P(MP, None), P(DP, None, MP)),
        check_vma=False,
    )
```
